512 devices in a mesh: rep: 8 (over y), shard: 64 (over x, z, core).
Axes of the slice: x: 4, y: 8, z: 8, core: 2. Of those that a mesh axis runs over, the one named last changes fastest.
Arguments:
- tokens_in: bfloat16 [8, 2048, 3072], P('rep', 'shard'), may hold values from -6 to 6
- grad_out: bfloat16 [8, 2048, 8192], P('rep', 'shard'), may hold values from -0.125 to 0.125
- error_old: float32 [8, 3072, 8192], P('rep', None, 'shard'), may hold values from -6 to 6
- q_prev: float32 [8192, 64], P('shard'), may hold values from -6 to 6
Outputs:
- approx: bfloat16 [3072, 8192], P(None, 'shard')
- new_error: float32 [8, 3072, 8192], P('rep', None, 'shard')
- q_new: float32 [8192, 64], P('shard')
The draws below stay inside these ranges and needn't reach their ends.
All inputs are finite; a program needn't handle non-finite values.
Results may differ from the reference program's by a relative error of at most 0.0014.
Values may be sent and summed in bfloat16 or wider, within the bound.
No kernel may reach another device: no remote copies, remote signals or barrier semaphores. Data moves between devices by JAX's collectives and lax.ppermute only.
A program may use at most 64 MiB of HBM per device.

```python
import jax
import jax.numpy as jnp
from jax import lax

ROWS = 3072
N = 8192
RANK = 64
GROUP_TOK = 2048
N_REP = 8


def levels(stream_key, dims, cuts, smallest, largest):
    gain, own = 1.0, jax.random.fold_in(stream_key, 6)
    for position, blocks in cuts:
        draws = jnp.exp(jax.random.uniform(jax.random.fold_in(own, position), (blocks,), jnp.float32, smallest / len(cuts), largest / len(cuts)))
        gain = gain * jnp.repeat(draws, dims[position] // blocks).reshape([-1 if axis == position else 1 for axis in range(len(dims))])
    return gain


def normal_values(key, dims, width, limit, cuts=(), dtype=jnp.bfloat16):
    loudness = levels(key, dims, cuts, -0.22, 0.18) if cuts else 1.0
    values = jax.random.normal(key, dims, jnp.float32) * width * loudness
    return jnp.minimum(jnp.maximum(values, -limit), limit).astype(dtype)


def setup_inputs(seed: int = 0) -> dict:
    streams_of = jax.random.split(jax.random.key(seed), 5)
    tokens_in = normal_values(streams_of[0], (N_REP, GROUP_TOK, ROWS), 1.0, 6.0, ((0, 8), (1, 64)))
    grad_out = normal_values(streams_of[1], (N_REP, GROUP_TOK, N), GROUP_TOK ** -0.5, 0.125, ((0, 8), (1, 64)))
    error_old = normal_values(streams_of[2], (N_REP, ROWS, N), 0.5, 6.0, ((0, 8), (2, 64)), jnp.float32)
    q_prev = normal_values(streams_of[3], (N, RANK), 1.0, 6.0, ((0, 64),), jnp.float32)
    return dict(tokens_in=tokens_in, grad_out=grad_out, error_old=error_old, q_prev=q_prev)


def reference(tokens_in, grad_out, error_old, q_prev):

    def one_group(pieces):
        inputs, outgrad, memory = pieces
        grad = jnp.dot(inputs.T.astype(jnp.float32), outgrad.astype(jnp.float32), preferred_element_type=jnp.float32)
        merged = grad + memory
        partial_left = jnp.dot(merged, q_prev, precision=lax.Precision.HIGHEST)
        return (merged, partial_left)
    merged, partials = lax.map(one_group, (tokens_in, grad_out, error_old))
    left = jnp.sum(partials, axis=0)
    gram = jnp.dot(left.T, left, precision=lax.Precision.HIGHEST)
    lower = jnp.linalg.cholesky(gram)
    basis = lax.linalg.triangular_solve(lower, left, left_side=False, lower=True, transpose_a=True)
    q_new = jnp.einsum('grn,rk->nk', merged, basis, precision=lax.Precision.HIGHEST) / N_REP
    approx_full = jnp.dot(basis, q_new.T, precision=lax.Precision.HIGHEST)
    new_error = merged - approx_full[None]
    return (approx_full.astype(jnp.bfloat16), new_error, q_new)
```

```python
import jax
import jax.numpy as jnp
from jax import lax
from jax.experimental import pallas as pl
from jax.experimental.pallas import tpu as pltpu
from jax.sharding import Mesh, PartitionSpec as P

F32 = jnp.float32
BF16 = jnp.bfloat16
HIGHEST = lax.Precision.HIGHEST
GROUP = ("x", "z")
PEERS = ("rep", "x", "core")
SWAP = [(0, 1), (1, 0)]
LANES = 128


def split(value):
    high = value.astype(BF16)
    return high, (value - high.astype(F32)).astype(BF16)


def dot_nt(a, b, precision=None):
    return lax.dot_general(a, b, (((1,), (1,)), ((), ())), precision=precision, preferred_element_type=F32)


def dot_nn(a, b, precision=None):
    return lax.dot_general(a, b, (((1,), (0,)), ((), ())), precision=precision, preferred_element_type=F32)


def dot_tn(a, b, precision=None):
    return lax.dot_general(a, b, (((0,), (0,)), ((), ())), precision=precision, preferred_element_type=F32)


def shaped(*shape, dtype=F32):
    return jax.ShapeDtypeStruct(shape, dtype)


def size_of(value):
    count = value.dtype.itemsize
    for extent in value.shape:
        count *= extent
    return count


def cost(flops, values):
    return pl.CostEstimate(flops=flops, bytes_accessed=sum(size_of(v) for v in values), transcendentals=0)


def vmem_call(body, out_shape, *args, flops=0, scratch=()):
    whole = pl.BlockSpec(memory_space=pltpu.VMEM)
    many = isinstance(out_shape, (tuple, list))
    return pl.pallas_call(
        body,
        out_shape=out_shape,
        in_specs=[whole] * len(args),
        out_specs=tuple(whole for _ in out_shape) if many else whole,
        scratch_shapes=scratch,
        cost_estimate=cost(flops, list(args) + (list(out_shape) if many else [out_shape])),
        compiler_params=pltpu.CompilerParams(vmem_limit_bytes=32 << 20),
    )(*args)


def steps_of(rows, step=512):
    step = min(rows, step)
    return [(start, step) for start in range(0, rows, step)]


def error_parts(q_ref, e_ref, left_ref, turned_ref):
    rank = q_ref.shape[0]
    q_high, q_low = split(q_ref[...])
    both = jnp.concatenate([q_high, q_low], axis=0)
    for start, step in steps_of(e_ref.shape[0]):
        cols = pl.ds(start, step)
        turned = e_ref[cols, :].T
        turned_ref[:, cols] = turned
        e_high, e_low = split(turned)
        wide = dot_nn(both, e_high)
        left_ref[:, cols] = wide[:rank] + (wide[rank:] + dot_nn(q_high, e_low))


def project(q_ref, q2_ref, cols_ref, out_ref, keep_ref, send_ref):
    rank = q_ref.shape[0]
    peers, _, count, _ = cols_ref.shape
    parts = []
    for ref in (q_ref, q2_ref):
        high, low = split(ref[...])
        parts.append(jnp.concatenate([high, low], axis=0))
    half = count // 2
    lane = lax.broadcasted_iota(jnp.int32, (half, LANES), 1)
    group = max(1, 128 // count)
    for j in range(0, peers, group):
        keep = cols_ref[j : j + group, 0].reshape(group * count, LANES)
        send = cols_ref[j : j + group, 1].reshape(group * count, LANES)
        wide = dot_nt(keep, parts[0]) + dot_nt(send, parts[1])
        value = wide + pltpu.roll(wide, rank, 1)
        for i in range(group):
            top = value[i * count : i * count + half]
            low = value[i * count + half : (i + 1) * count]
            out_ref[j + i] = jnp.where(lane < rank, top, low)
        cols = pl.ds(j * count, group * count)
        keep_ref[:, cols] = keep.astype(F32).T.astype(BF16)
        send_ref[:, cols] = send.astype(F32).T.astype(BF16)


def token_left(y_ref, tok_ref, add_ref, out_ref):
    rank = add_ref.shape[0]
    packed = jnp.sum(y_ref[...], axis=0)
    value = jnp.concatenate([packed, pltpu.roll(packed, rank, 1)], axis=0)
    high, low = split(value.T[:rank])
    both = jnp.concatenate([high, low], axis=0)
    bands = rank // 8
    blocks = out_ref.shape[0] // bands
    width = out_ref.shape[2]
    for c in range(blocks):
        cols = pl.ds(c * width, width)
        wide = dot_nn(both, tok_ref[:, cols])
        total = add_ref[:, cols] + (wide[:rank] + wide[rank:])
        for b in range(bands):
            out_ref[b * blocks + c] = total[b * 8 : (b + 1) * 8]


def unblock(left_ref, rank, c):
    bands = rank // 8
    blocks = left_ref.shape[0] // bands
    return jnp.concatenate([left_ref[b * blocks + c] for b in range(bands)], axis=0)


def left_forms(left_ref, wide_ref, tall_ref):
    rank = wide_ref.shape[0] // 2
    width = left_ref.shape[2]
    for c in range(wide_ref.shape[1] // width):
        high, low = split(unblock(left_ref, rank, c))
        both = jnp.concatenate([high, low], axis=0)
        cols = pl.ds(c * width, width)
        wide_ref[:, cols] = both
        tall_ref[cols, :] = both.astype(F32).T.astype(BF16)


def inverse_factor(left_ref, out_ref):
    rank = out_ref.shape[0]
    width = left_ref.shape[2]
    gram = jnp.zeros((rank, rank), F32)
    for c in range(left_ref.shape[0] // (rank // 8)):
        block = unblock(left_ref, rank, c)
        gram += dot_nt(block, block, HIGHEST)
    row_at = lax.broadcasted_iota(jnp.int32, (rank, rank), 0)
    col_at = lax.broadcasted_iota(jnp.int32, (rank, rank), 1)
    work = jnp.concatenate([gram, (row_at == col_at).astype(F32)], axis=1)
    tiles = [work[i * 8 : (i + 1) * 8] for i in range(rank // 8)]
    below = lax.broadcasted_iota(jnp.int32, (8, 1), 0)
    done = []
    for k in range(rank):
        at, sub = divmod(k, 8)
        row = tiles[at][sub : sub + 1, :]
        pivot = row[:, k : k + 1]
        scaled = row / pivot
        done.append(row * lax.rsqrt(pivot))
        for i in range(at, rank // 8):
            column = tiles[i][:, k : k + 1]
            if i == at:
                column = jnp.where(below > sub, column, 0.0)
            tiles[i] = tiles[i] - column * scaled
    out_ref[...] = jnp.concatenate(done, axis=0)[:, rank:]


def columns_product(cols_ref, tok_ref, out_ref):
    out_ref[...] = dot_nn(cols_ref[...], tok_ref[...])


def turned_grad(columns, gathered):
    own, tokens = columns.shape
    rows = gathered.shape[1]
    step = min(rows, 512)
    return pl.pallas_call(
        columns_product,
        out_shape=shaped(own, rows),
        grid=(rows // step,),
        in_specs=[
            pl.BlockSpec((own, tokens), lambda i: (0, 0)),
            pl.BlockSpec((tokens, step), lambda i: (0, i)),
        ],
        out_specs=pl.BlockSpec((own, step), lambda i: (0, i)),
        cost_estimate=cost(2 * own * tokens * rows, [columns, gathered]),
        compiler_params=pltpu.CompilerParams(vmem_limit_bytes=32 << 20),
    )(columns, gathered)


def merge(keep_ref, in_ref, e_ref, left_ref, merged_ref, right_ref):
    rank = left_ref.shape[0] // 2
    own, rows = keep_ref.shape
    top = jnp.zeros((2 * rank, own), F32)
    low = jnp.zeros((rank, own), F32)
    for start, step in steps_of(rows):
        cols = pl.ds(start, step)
        merged = (keep_ref[:, cols] + in_ref[:, cols]) + e_ref[:, cols]
        merged_ref[:, cols] = merged
        m_high, m_low = split(merged)
        top += dot_nt(left_ref[:, cols], m_high)
        low += dot_nt(left_ref[:rank, cols], m_low)
    right = top[:rank] + (top[rank:] + low)
    for g in range(right_ref.shape[0]):
        right_ref[g] = right


def turn(in_ref, out_ref):
    for start, step in steps_of(in_ref.shape[1]):
        out_ref[pl.ds(start, step), :] = in_ref[:, pl.ds(start, step)].T


def finish(right_ref, inverse_ref, left_ref, merged_ref, approx_ref, error_ref, q_ref):
    rank = inverse_ref.shape[0]
    reps = right_ref.shape[0]
    inverse = inverse_ref[...]
    right = jnp.sum(right_ref[...], axis=0)
    q_new = dot_nn(inverse, right, HIGHEST) / reps
    q_ref[...] = q_new
    high, low = split(dot_tn(inverse, q_new, HIGHEST))
    first = jnp.concatenate([high, high], axis=0)
    second = jnp.concatenate([low, jnp.zeros_like(low)], axis=0)
    left = left_ref[...]
    approx = dot_nn(left, first) + dot_nn(left, second)
    approx_ref[...] = approx.astype(BF16)
    error_ref[...] = merged_ref[...] - approx


def finished(right, inverse, left, merged):
    rows, own = merged.shape
    rank = inverse.shape[0]
    step = min(rows, 768)
    same = lambda i: (0, 0)
    block = lambda i: (i, 0)
    outs = (shaped(rows, own, dtype=BF16), shaped(rows, own), shaped(rank, own))
    return pl.pallas_call(
        finish,
        out_shape=outs,
        grid=(rows // step,),
        in_specs=[
            pl.BlockSpec(right.shape, lambda i: (0, 0, 0)),
            pl.BlockSpec(inverse.shape, same),
            pl.BlockSpec((step, 2 * rank), block),
            pl.BlockSpec((step, own), block),
        ],
        out_specs=(
            pl.BlockSpec((step, own), block),
            pl.BlockSpec((step, own), block),
            pl.BlockSpec((rank, own), same),
        ),
        cost_estimate=cost(6 * rows * rank * own, [right, left, merged] + list(outs)),
        compiler_params=pltpu.CompilerParams(vmem_limit_bytes=32 << 20),
    )(right, inverse, left, merged)


def direct(blocks, axes):
    return lax.all_to_all(blocks, axes, split_axis=0, concat_axis=0, tiled=True)


def spread(block, axes, count):
    return direct(jnp.broadcast_to(block[None], (count,) + block.shape), axes)


def per_device(sizes, tokens_in, grad_out, error_old, q_prev):
    tokens, outgrad, memory = tokens_in[0], grad_out[0], error_old[0]
    count, rows = tokens.shape
    own, rank = q_prev.shape
    members = sizes["x"] * sizes["z"]
    peers = sizes["rep"] * sizes["x"] * sizes["core"]
    core = lax.axis_index("core")

    gathered = lax.all_gather(tokens, GROUP, axis=0, tiled=True)
    q_t = q_prev.T
    q_t2 = lax.ppermute(q_t, "core", SWAP)
    cut = outgrad.reshape(count, members, 2, own).transpose(1, 2, 0, 3)
    cut = jnp.where(core == 0, cut, cut[:, ::-1])
    columns = direct(cut, GROUP)
    left_part, memory_t = vmem_call(
        error_parts, (shaped(rank, rows), shaped(own, rows)), q_t, memory, flops=6 * rank * rows * own
    )
    projected, keep, send = vmem_call(
        project,
        (
            shaped(members, count // 2, own),
            shaped(own, members * count, dtype=BF16),
            shaped(own, members * count, dtype=BF16),
        ),
        q_t,
        q_t2,
        columns,
        flops=8 * rank * own * members * count,
    )
    projected = direct(projected, GROUP)
    width = rows * rank // (8 * peers)
    left = vmem_call(token_left, shaped(peers, 8, width), projected, tokens, left_part, flops=4 * rank * count * rows)

    left = direct(left, PEERS).sum(0)
    left = spread(left, "z", sizes["z"]).sum(0)
    left = spread(left, PEERS, peers)

    left_wide, left_tall = vmem_call(
        left_forms, (shaped(2 * rank, rows, dtype=BF16), shaped(rows, 2 * rank, dtype=BF16)), left
    )
    inverse = vmem_call(inverse_factor, shaped(rank, rank), left, flops=12 * rank * rank * rows)

    grad_send = turned_grad(send, gathered)
    grad_in = lax.ppermute(grad_send, "core", SWAP)
    grad_keep = turned_grad(keep, gathered)
    merged_t, right = vmem_call(
        merge,
        (shaped(own, rows), shaped(sizes["rep"], rank, own)),
        grad_keep,
        grad_in,
        memory_t,
        left_wide,
        flops=6 * rank * own * rows,
    )
    right = direct(right, "rep")
    merged = vmem_call(turn, shaped(rows, own), merged_t)
    approx, new_error, q_new = finished(right, inverse, left_tall, merged)
    return approx, new_error[None], q_new.T


def solution(mesh):
    return build(mesh, (8, 4, 8, 2))


def build(mesh, shape):
    names = ("rep", "x", "z", "core")
    grid = Mesh(mesh.devices.reshape(shape), names)
    sizes = dict(zip(names, shape))
    shard = ("x", "z", "core")
    placed = (
        P("rep", shard, None),
        P("rep", shard, None),
        P("rep", None, shard),
        P(shard, None),
    )
    return jax.shard_map(
        lambda *args: per_device(sizes, *args),
        mesh=grid,
        in_specs=placed,
        out_specs=(P(None, shard), P("rep", None, shard), P(shard, None)),
        check_vma=False,
    )
```

```python
import jax
import jax.numpy as jnp
from jax import lax
from jax.experimental import pallas as pl
from jax.experimental.pallas import tpu as pltpu
from jax.sharding import Mesh, PartitionSpec as P

F32 = jnp.float32
BF16 = jnp.bfloat16
HIGHEST = lax.Precision.HIGHEST
PEERS = ("rep", "x")
SWAP = [(0, 1), (1, 0)]
LANES = 128


def split(value):
    high = value.astype(BF16)
    return high, (value - high.astype(F32)).astype(BF16)


def dot_nt(a, b, precision=None):
    return lax.dot_general(a, b, (((1,), (1,)), ((), ())), precision=precision, preferred_element_type=F32)


def dot_nn(a, b, precision=None):
    return lax.dot_general(a, b, (((1,), (0,)), ((), ())), precision=precision, preferred_element_type=F32)


def dot_tn(a, b, precision=None):
    return lax.dot_general(a, b, (((0,), (0,)), ((), ())), precision=precision, preferred_element_type=F32)


def shaped(*shape, dtype=F32):
    return jax.ShapeDtypeStruct(shape, dtype)


def size_of(value):
    count = value.dtype.itemsize
    for extent in value.shape:
        count *= extent
    return count


def cost(flops, values):
    return pl.CostEstimate(flops=flops, bytes_accessed=sum(size_of(v) for v in values), transcendentals=0)


def vmem_call(body, out_shape, *args, flops=0, scratch=(), extra=0):
    whole = pl.BlockSpec(memory_space=pltpu.VMEM)
    many = isinstance(out_shape, (tuple, list))
    values = list(args) + (list(out_shape) if many else [out_shape])
    room = sum(size_of(v) for v in values) + extra
    return pl.pallas_call(
        body,
        out_shape=out_shape,
        in_specs=[whole] * len(args),
        out_specs=tuple(whole for _ in out_shape) if many else whole,
        scratch_shapes=scratch,
        cost_estimate=cost(flops, values),
        compiler_params=pltpu.CompilerParams(vmem_limit_bytes=room + (6 << 20)),
    )(*args)


def steps_of(rows, step=512):
    step = min(rows, step)
    return [(start, step) for start in range(0, rows, step)]


def error_parts(q_ref, e_ref, tok_ref, left_ref, turned_ref):
    rank = q_ref.shape[0]
    q_high, q_low = split(q_ref[...])
    both = jnp.concatenate([q_high, q_low], axis=0)
    for start, step in steps_of(e_ref.shape[0]):
        cols = pl.ds(start, step)
        turned = e_ref[cols, :].T
        turned_ref[:, cols] = turned
        e_high, e_low = split(turned)
        wide = dot_nn(both, e_high)
        left_ref[:rank, cols] = wide[:rank] + (wide[rank:] + dot_nn(q_high, e_low))
        left_ref[rank:, cols] = tok_ref[:, cols].astype(F32)


def cut_columns(in_ref, out_ref):
    deep, across, _, own = out_ref.shape
    for z in range(deep):
        for i in range(across):
            x, core = divmod(i, 2)
            start = ((x * deep + z) * 2 + core) * own
            out_ref[z, i] = in_ref[:, start : start + own]


def pack_factor(*refs):
    *q_refs, out_ref = refs
    across, rank = len(q_refs), q_refs[0].shape[1]
    x, core = lax.axis_index("x"), lax.axis_index("core")
    for shift, q_ref in enumerate(q_refs):
        source = lax.rem(x + across - shift, across)
        for i in (0, 1):
            high, low = split(q_ref[i])
            place = 2 * source + (core if i == 0 else 1 - core)
            out_ref[place] = jnp.concatenate([high, low], axis=0)


def project(q_ref, cols_ref, out_ref):
    near, wide, own = q_ref.shape
    rank = wide // 2
    deep, _, count, _ = cols_ref.shape
    total = jnp.zeros((deep * count, wide), F32)
    for i in range(near):
        total += dot_nt(cols_ref[:, i].reshape(deep * count, own), q_ref[i])
    value = total + pltpu.roll(total, rank, 1)
    half = count // 2
    lane = lax.broadcasted_iota(jnp.int32, (half, 2 * rank), 1)
    for z in range(deep):
        top = value[z * count : z * count + half]
        low = value[z * count + half : (z + 1) * count]
        packed = jnp.where(lane < rank, top, low)
        out_ref[2 * z] = packed
        out_ref[2 * z + 1] = packed


def pick_columns(cols_ref, *out_refs):
    across = len(out_refs)
    x = lax.axis_index("x")
    for shift, out_ref in enumerate(out_refs):
        out_ref[...] = cols_ref[:, pl.ds(2 * lax.rem(x + shift, across), 2)]


def turn_columns(*refs):
    *in_refs, out_ref = refs
    deep, _, count, own = in_refs[0].shape
    across = len(in_refs)
    x, core = lax.axis_index("x"), lax.axis_index("core")
    for shift, in_ref in enumerate(in_refs):
        source = lax.rem(x + across - shift, across)
        cols = pl.ds(pl.multiple_of(source * (deep * count), deep * count), deep * count)
        for i in (0, 1):
            block = in_ref[:, core if i == 0 else 1 - core].reshape(deep * count, own)
            out_ref[i * own : (i + 1) * own, cols] = block.astype(F32).T.astype(BF16)


def token_left(y_ref, add_ref, add2_ref, out_ref):
    rank, rows = y_ref.shape[2] // 2, add_ref.shape[1]
    core = lax.axis_index("core")
    packed = [y_ref[i] for i in (0, 1)]
    for z in range(1, y_ref.shape[0] // 2):
        packed = [packed[i] + y_ref[2 * z + i] for i in (0, 1)]
    ordered = [jnp.where(core == i, packed[0], packed[1]) for i in (0, 1)]
    value = jnp.concatenate(
        [part for one in ordered for part in (one, pltpu.roll(one, rank, 1))], axis=0
    )
    high, low = split(value.T[:rank])
    both = jnp.concatenate([high, low], axis=0)
    bands = rank // 8
    blocks = out_ref.shape[0] // bands
    width = out_ref.shape[2]
    for c in range(blocks):
        cols = pl.ds(pl.multiple_of(core * (rows // 2) + c * width, LANES), width)
        pair = jnp.concatenate([add_ref[rank:, cols], add2_ref[rank:, cols]], axis=0).astype(BF16)
        wide = dot_nn(both, pair)
        total = (add_ref[:rank, cols] + add2_ref[:rank, cols]) + (wide[:rank] + wide[rank:])
        for b in range(bands):
            out_ref[b * blocks + c] = total[b * 8 : (b + 1) * 8]


def add_spread(in_ref, out_ref):
    total = jnp.sum(in_ref[...], axis=0)
    for i in range(out_ref.shape[0]):
        out_ref[i] = total


def unblock(left_ref, rank, c):
    bands = rank // 8
    blocks = left_ref.shape[0] // bands
    return jnp.concatenate([left_ref[b * blocks + c] for b in range(bands)], axis=0)


def left_forms(mine_ref, other_ref, wide_ref, tall_ref):
    rank = wide_ref.shape[0] // 2
    rows = wide_ref.shape[1]
    width = mine_ref.shape[2]
    core = lax.axis_index("core")
    for ref, place in ((mine_ref, core), (other_ref, 1 - core)):
        for c in range(rows // 2 // width):
            high, low = split(unblock(ref, rank, c))
            both = jnp.concatenate([high, low], axis=0)
            cols = pl.ds(pl.multiple_of(place * (rows // 2) + c * width, LANES), width)
            wide_ref[:, cols] = both
            tall_ref[cols, :] = both.astype(F32).T.astype(BF16)


def inverse_factor(mine_ref, other_ref, out_ref):
    rank = out_ref.shape[0]
    grams = []
    for ref in (mine_ref, other_ref):
        gram = jnp.zeros((rank, rank), F32)
        for c in range(ref.shape[0] // (rank // 8)):
            block = unblock(ref, rank, c)
            gram += dot_nt(block, block, HIGHEST)
        grams.append(gram)
    gram = grams[0] + grams[1]
    row_at = lax.broadcasted_iota(jnp.int32, (rank, rank), 0)
    col_at = lax.broadcasted_iota(jnp.int32, (rank, rank), 1)
    work = jnp.concatenate([gram, (row_at == col_at).astype(F32)], axis=1)
    tiles = [work[i * 8 : (i + 1) * 8] for i in range(rank // 8)]
    below = lax.broadcasted_iota(jnp.int32, (8, 1), 0)
    done = []
    for k in range(rank):
        at, sub = divmod(k, 8)
        row = tiles[at][sub : sub + 1, :]
        pivot = row[:, k : k + 1]
        scaled = row / pivot
        done.append(row * lax.rsqrt(pivot))
        for i in range(at, rank // 8):
            column = tiles[i][:, k : k + 1]
            if i == at:
                column = jnp.where(below > sub, column, 0.0)
            tiles[i] = tiles[i] - column * scaled
    out_ref[...] = jnp.concatenate(done, axis=0)[:, rank:]


def turned_grad(cols_ref, e_ref, tok_ref, keep_ref, send_ref):
    own = keep_ref.shape[0]
    for start, step in steps_of(tok_ref.shape[1]):
        cols = pl.ds(start, step)
        both = dot_nn(cols_ref[...], tok_ref[:, cols])
        send_ref[:, cols] = both[own:]
        keep_ref[:, cols] = both[:own] + e_ref[:, cols]


def merge(keep_ref, in_ref, left_ref, merged_ref, right_ref):
    rank = left_ref.shape[0] // 2
    own, rows = keep_ref.shape
    top = jnp.zeros((2 * rank, own), F32)
    low = jnp.zeros((rank, own), F32)
    for start, step in steps_of(rows):
        cols = pl.ds(start, step)
        merged = keep_ref[:, cols] + in_ref[:, cols]
        merged_ref[:, cols] = merged
        m_high, m_low = split(merged)
        top += dot_nt(left_ref[:, cols], m_high)
        low += dot_nt(left_ref[:rank, cols], m_low)
    right = top[:rank] + (top[rank:] + low)
    for g in range(right_ref.shape[0]):
        right_ref[g] = right


def turn(in_ref, out_ref):
    for start, step in steps_of(in_ref.shape[1]):
        out_ref[pl.ds(start, step), :] = in_ref[:, pl.ds(start, step)].T


def finish(right_ref, inverse_ref, left_ref, merged_ref, approx_ref, error_ref, q_ref, weights):
    rank, own = q_ref.shape
    reps = right_ref.shape[0]

    @pl.when(pl.program_id(0) == 0)
    def _():
        inverse = inverse_ref[...]
        right = jnp.sum(right_ref[...], axis=0)
        q_new = dot_nn(inverse, right, HIGHEST) / reps
        q_ref[...] = q_new
        high, low = split(dot_tn(inverse, q_new, HIGHEST))
        weights[:rank, :own] = high
        weights[rank:, :own] = high
        weights[:rank, own:] = low
        weights[rank:, own:] = jnp.zeros_like(low)

    wide = dot_nn(left_ref[...], weights[...])
    approx = wide[:, :own] + wide[:, own:]
    approx_ref[...] = approx.astype(BF16)
    error_ref[...] = merged_ref[...] - approx


def finished(right, inverse, left, merged):
    rows, own = merged.shape
    rank = inverse.shape[0]
    step = min(rows, 768)
    same = lambda i: (0, 0)
    block = lambda i: (i, 0)
    outs = (shaped(rows, own, dtype=BF16), shaped(rows, own), shaped(rank, own))
    return pl.pallas_call(
        finish,
        out_shape=outs,
        grid=(rows // step,),
        in_specs=[
            pl.BlockSpec(right.shape, lambda i: (0, 0, 0)),
            pl.BlockSpec(inverse.shape, same),
            pl.BlockSpec((step, 2 * rank), block),
            pl.BlockSpec((step, own), block),
        ],
        out_specs=(
            pl.BlockSpec((step, own), block),
            pl.BlockSpec((step, own), block),
            pl.BlockSpec((rank, own), same),
        ),
        scratch_shapes=[pltpu.VMEM((2 * rank, 2 * own), BF16)],
        cost_estimate=cost(6 * rows * rank * own, [right, left, merged] + list(outs)),
        compiler_params=pltpu.CompilerParams(vmem_limit_bytes=60 << 20),
    )(right, inverse, left, merged)


def direct(blocks, axes):
    return lax.all_to_all(blocks, axes, split_axis=0, concat_axis=0, tiled=True)


def shifted(value, across, shift):
    return lax.ppermute(value, "x", [(i, (i + shift) % across) for i in range(across)])


def after(value, earlier):
    return lax.optimization_barrier((value, earlier))[0]


def per_device(sizes, tokens_in, grad_out, error_old, q_prev):
    tokens, outgrad, memory = tokens_in[0], grad_out[0], error_old[0]
    count, rows = tokens.shape
    own, rank = q_prev.shape
    reps, across, deep = sizes["rep"], sizes["x"], sizes["z"]
    peers = reps * across
    width = rows * rank // (16 * peers)

    gathered = lax.all_gather(tokens, ("x", "z"), axis=0, tiled=True)
    q_t = q_prev.T
    cut = vmem_call(cut_columns, shaped(deep, across * 2, count, own, dtype=BF16), outgrad)
    q_t, memory = lax.optimization_barrier((q_t, memory, cut))[:2]
    cut = direct(cut, "z")
    q_pair = jnp.stack([q_t, lax.ppermute(q_t, "core", SWAP)])
    q_near = [q_pair] + [shifted(q_pair, across, s) for s in range(1, across)]
    left_own, memory_t = vmem_call(
        error_parts,
        (shaped(rank + count, rows), shaped(own, rows)),
        q_t,
        memory,
        tokens,
        flops=6 * rank * rows * own,
    )
    q_near = vmem_call(pack_factor, shaped(2 * across, 2 * rank, own, dtype=BF16), *q_near)
    projected = vmem_call(
        project,
        shaped(deep * 2, count // 2, own),
        q_near,
        cut,
        flops=4 * rank * own * deep * across * 2 * count,
    )
    left_own2 = lax.ppermute(after(left_own, projected), "core", SWAP)
    projected = direct(projected, ("z", "core"))
    left = vmem_call(
        token_left,
        shaped(peers, 8, width),
        projected,
        left_own,
        left_own2,
        flops=4 * rank * count * rows,
    )
    late_cut = after(cut, left)
    chip = shaped(deep, 2, count, own, dtype=BF16)
    columns = vmem_call(pick_columns, (chip,) * across, late_cut)
    columns = [columns[0]] + [shifted(columns[s], across, s) for s in range(1, across)]
    columns = vmem_call(
        turn_columns,
        shaped(2 * own, deep * across * count, dtype=BF16),
        *columns,
    )
    left = direct(left, PEERS)
    left = vmem_call(add_spread, shaped(deep, 8, width), after(left, columns))
    left = direct(left, "z")
    summed = vmem_call(add_spread, shaped(peers, 8, width), left)
    left = direct(summed, PEERS)
    gathered = after(gathered, summed)
    grad_keep, grad_send = vmem_call(
        turned_grad,
        (shaped(own, rows), shaped(own, rows)),
        columns,
        memory_t,
        gathered,
        flops=4 * own * rows * deep * across * count,
    )
    grad_in = lax.ppermute(grad_send, "core", SWAP)

    left2 = lax.ppermute(after(left, grad_send), "core", SWAP)

    left_wide, left_tall = vmem_call(
        left_forms, (shaped(2 * rank, rows, dtype=BF16), shaped(rows, 2 * rank, dtype=BF16)), left, left2
    )
    inverse = vmem_call(inverse_factor, shaped(rank, rank), left, left2, flops=12 * rank * rank * rows)
    merged_t, right = vmem_call(
        merge,
        (shaped(own, rows), shaped(reps, rank, own)),
        grad_keep,
        grad_in,
        left_wide,
        flops=6 * rank * own * rows,
    )
    right = direct(right, "rep")
    merged = vmem_call(turn, shaped(rows, own), merged_t)
    approx, new_error, q_new = finished(right, inverse, left_tall, merged)
    return approx, new_error[None], q_new.T


def solution(mesh):
    return build(mesh, (8, 4, 8, 2))


def build(mesh, shape):
    names = ("rep", "x", "z", "core")
    grid = Mesh(mesh.devices.reshape(shape), names)
    sizes = dict(zip(names, shape))
    shard = ("x", "z", "core")
    placed = (
        P("rep", shard, None),
        P("rep", shard, None),
        P("rep", None, shard),
        P(shard, None),
    )
    return jax.shard_map(
        lambda *args: per_device(sizes, *args),
        mesh=grid,
        in_specs=placed,
        out_specs=(P(None, shard), P("rep", None, shard), P(shard, None)),
        check_vma=False,
    )
```

```python
import jax
import jax.numpy as jnp
from jax import lax
from jax.experimental import pallas as pl
from jax.experimental.pallas import tpu as pltpu
from jax.sharding import Mesh, PartitionSpec as P

F32 = jnp.float32
BF16 = jnp.bfloat16
HIGHEST = lax.Precision.HIGHEST
PEERS = ("rep", "x")
SWAP = [(0, 1), (1, 0)]
LANES = 128


def split(value):
    high = value.astype(BF16)
    return high, (value - high.astype(F32)).astype(BF16)


def dot_nt(a, b, precision=None):
    return lax.dot_general(a, b, (((1,), (1,)), ((), ())), precision=precision, preferred_element_type=F32)


def dot_nn(a, b, precision=None):
    return lax.dot_general(a, b, (((1,), (0,)), ((), ())), precision=precision, preferred_element_type=F32)


def dot_tn(a, b, precision=None):
    return lax.dot_general(a, b, (((0,), (0,)), ((), ())), precision=precision, preferred_element_type=F32)


def shaped(*shape, dtype=F32):
    return jax.ShapeDtypeStruct(shape, dtype)


def size_of(value):
    count = value.dtype.itemsize
    for extent in value.shape:
        count *= extent
    return count


def cost(flops, values):
    return pl.CostEstimate(flops=flops, bytes_accessed=sum(size_of(v) for v in values), transcendentals=0)


def vmem_call(body, out_shape, *args, flops=0, scratch=(), extra=0):
    whole = pl.BlockSpec(memory_space=pltpu.VMEM)
    many = isinstance(out_shape, (tuple, list))
    values = list(args) + (list(out_shape) if many else [out_shape])
    room = sum(size_of(v) for v in values) + extra
    return pl.pallas_call(
        body,
        out_shape=out_shape,
        in_specs=[whole] * len(args),
        out_specs=tuple(whole for _ in out_shape) if many else whole,
        scratch_shapes=scratch,
        cost_estimate=cost(flops, values),
        compiler_params=pltpu.CompilerParams(vmem_limit_bytes=room + (6 << 20)),
    )(*args)


def steps_of(rows, step=512):
    step = min(rows, step)
    return [(start, step) for start in range(0, rows, step)]


def error_parts(q_ref, e_ref, tok_ref, left_ref, turned_ref):
    rank = q_ref.shape[0]
    q_high, q_low = split(q_ref[...])
    both = jnp.concatenate([q_high, q_low], axis=0)
    for start, step in steps_of(e_ref.shape[0]):
        cols = pl.ds(start, step)
        turned = e_ref[cols, :].T
        turned_ref[:, cols] = turned
        e_high, e_low = split(turned)
        wide = dot_nn(both, e_high)
        left_ref[:rank, cols] = wide[:rank] + (wide[rank:] + dot_nn(q_high, e_low))
        left_ref[rank:, cols] = tok_ref[:, cols].astype(F32)


def cut_columns(in_ref, out_ref):
    deep, across, _, own = out_ref.shape
    for z in range(deep):
        for i in range(across):
            x, core = divmod(i, 2)
            start = ((x * deep + z) * 2 + core) * own
            out_ref[z, i] = in_ref[:, start : start + own]


def pack_factor(*refs):
    *q_refs, out_ref = refs
    across, rank = len(q_refs), q_refs[0].shape[1]
    x, core = lax.axis_index("x"), lax.axis_index("core")
    for shift, q_ref in enumerate(q_refs):
        source = lax.rem(x + across - shift, across)
        for i in (0, 1):
            high, low = split(q_ref[i])
            place = 2 * source + (core if i == 0 else 1 - core)
            out_ref[place] = jnp.concatenate([high, low], axis=0)


def project(q_ref, cols_ref, out_ref):
    near, wide, own = q_ref.shape
    rank = wide // 2
    deep, _, count, _ = cols_ref.shape
    total = jnp.zeros((deep * count, wide), F32)
    for i in range(near):
        total += dot_nt(cols_ref[:, i].reshape(deep * count, own), q_ref[i])
    value = total + pltpu.roll(total, rank, 1)
    half = count // 2
    lane = lax.broadcasted_iota(jnp.int32, (half, 2 * rank), 1)
    for z in range(deep):
        top = value[z * count : z * count + half]
        low = value[z * count + half : (z + 1) * count]
        packed = jnp.where(lane < rank, top, low)
        out_ref[2 * z] = packed
        out_ref[2 * z + 1] = packed


def pick_columns(cols_ref, *out_refs):
    across = len(out_refs)
    x = lax.axis_index("x")
    for shift, out_ref in enumerate(out_refs):
        out_ref[...] = cols_ref[:, pl.ds(2 * lax.rem(x + shift, across), 2)]


def turn_columns(*refs):
    *in_refs, out_ref = refs
    deep, _, count, own = in_refs[0].shape
    across = len(in_refs)
    x, core = lax.axis_index("x"), lax.axis_index("core")
    for shift, in_ref in enumerate(in_refs):
        source = lax.rem(x + across - shift, across)
        cols = pl.ds(pl.multiple_of(source * (deep * count), deep * count), deep * count)
        for i in (0, 1):
            block = in_ref[:, core if i == 0 else 1 - core].reshape(deep * count, own)
            out_ref[i * own : (i + 1) * own, cols] = block.astype(F32).T.astype(BF16)


def token_left(y_ref, add_ref, add2_ref, out_ref):
    rank, rows = y_ref.shape[2] // 2, add_ref.shape[1]
    core = lax.axis_index("core")
    packed = [y_ref[i] for i in (0, 1)]
    for z in range(1, y_ref.shape[0] // 2):
        packed = [packed[i] + y_ref[2 * z + i] for i in (0, 1)]
    ordered = [jnp.where(core == i, packed[0], packed[1]) for i in (0, 1)]
    value = jnp.concatenate(
        [part for one in ordered for part in (one, pltpu.roll(one, rank, 1))], axis=0
    )
    high, low = split(value.T[:rank])
    both = jnp.concatenate([high, low], axis=0)
    bands = rank // 8
    blocks = out_ref.shape[0] // bands
    width = out_ref.shape[2]
    for c in range(blocks):
        cols = pl.ds(pl.multiple_of(core * (rows // 2) + c * width, LANES), width)
        pair = jnp.concatenate([add_ref[rank:, cols], add2_ref[rank:, cols]], axis=0).astype(BF16)
        wide = dot_nn(both, pair)
        total = (add_ref[:rank, cols] + add2_ref[:rank, cols]) + (wide[:rank] + wide[rank:])
        for b in range(bands):
            out_ref[b * blocks + c] = total[b * 8 : (b + 1) * 8]


def add_spread(in_ref, out_ref):
    total = jnp.sum(in_ref[...], axis=0)
    for i in range(out_ref.shape[0]):
        out_ref[i] = total


def unblock(left_ref, rank, c):
    bands = rank // 8
    blocks = left_ref.shape[0] // bands
    return jnp.concatenate([left_ref[b * blocks + c] for b in range(bands)], axis=0)


def left_forms(mine_ref, other_ref, wide_ref, tall_ref):
    rank = wide_ref.shape[0] // 2
    rows = wide_ref.shape[1]
    width = mine_ref.shape[2]
    core = lax.axis_index("core")
    for ref, place in ((mine_ref, core), (other_ref, 1 - core)):
        for c in range(rows // 2 // width):
            high, low = split(unblock(ref, rank, c))
            both = jnp.concatenate([high, low], axis=0)
            cols = pl.ds(pl.multiple_of(place * (rows // 2) + c * width, LANES), width)
            wide_ref[:, cols] = both
            tall_ref[cols, :] = both.astype(F32).T.astype(BF16)


def inverse_factor(mine_ref, other_ref, out_ref):
    rank = out_ref.shape[0]
    grams = []
    for ref in (mine_ref, other_ref):
        gram = jnp.zeros((rank, rank), F32)
        for c in range(ref.shape[0] // (rank // 8)):
            block = unblock(ref, rank, c)
            gram += dot_nt(block, block, HIGHEST)
        grams.append(gram)
    gram = grams[0] + grams[1]
    row_at = lax.broadcasted_iota(jnp.int32, (rank, rank), 0)
    col_at = lax.broadcasted_iota(jnp.int32, (rank, rank), 1)
    work = jnp.concatenate([gram, (row_at == col_at).astype(F32)], axis=1)
    tiles = [work[i * 8 : (i + 1) * 8] for i in range(rank // 8)]
    below = lax.broadcasted_iota(jnp.int32, (8, 1), 0)
    done = []
    for k in range(rank):
        at, sub = divmod(k, 8)
        row = tiles[at][sub : sub + 1, :]
        pivot = row[:, k : k + 1]
        scaled = row / pivot
        done.append(row * lax.rsqrt(pivot))
        for i in range(at, rank // 8):
            column = tiles[i][:, k : k + 1]
            if i == at:
                column = jnp.where(below > sub, column, 0.0)
            tiles[i] = tiles[i] - column * scaled
    out_ref[...] = jnp.concatenate(done, axis=0)[:, rank:]


def turned_grad(cols_ref, e_ref, tok_ref, keep_ref, send_ref):
    own = keep_ref.shape[0]
    for start, step in steps_of(tok_ref.shape[1]):
        cols = pl.ds(start, step)
        both = dot_nn(cols_ref[...], tok_ref[:, cols])
        send_ref[:, cols] = both[own:]
        keep_ref[:, cols] = both[:own] + e_ref[:, cols]


def merge(keep_ref, in_ref, left_ref, merged_ref, right_ref):
    rank = left_ref.shape[0] // 2
    own, rows = keep_ref.shape
    top = jnp.zeros((2 * rank, own), F32)
    low = jnp.zeros((rank, own), F32)
    for start, step in steps_of(rows):
        cols = pl.ds(start, step)
        merged = keep_ref[:, cols] + in_ref[:, cols]
        merged_ref[:, cols] = merged
        m_high, m_low = split(merged)
        top += dot_nt(left_ref[:, cols], m_high)
        low += dot_nt(left_ref[:rank, cols], m_low)
    right = top[:rank] + (top[rank:] + low)
    for g in range(right_ref.shape[0]):
        right_ref[g] = right


def turn(in_ref, out_ref):
    for start, step in steps_of(in_ref.shape[1]):
        out_ref[pl.ds(start, step), :] = in_ref[:, pl.ds(start, step)].T


def finish(right_ref, inverse_ref, left_ref, merged_ref, approx_ref, error_ref, q_ref, weights):
    rank, own = q_ref.shape
    reps = right_ref.shape[0]

    @pl.when(pl.program_id(0) == 0)
    def _():
        inverse = inverse_ref[...]
        right = jnp.sum(right_ref[...], axis=0)
        q_new = dot_nn(inverse, right, HIGHEST) / reps
        q_ref[...] = q_new
        high, low = split(dot_tn(inverse, q_new, HIGHEST))
        weights[:rank, :own] = high
        weights[rank:, :own] = high
        weights[:rank, own:] = low
        weights[rank:, own:] = jnp.zeros_like(low)

    wide = dot_nn(left_ref[...], weights[...])
    approx = wide[:, :own] + wide[:, own:]
    approx_ref[...] = approx.astype(BF16)
    error_ref[...] = merged_ref[...] - approx


def finished(right, inverse, left, merged):
    rows, own = merged.shape
    rank = inverse.shape[0]
    step = min(rows, 768)
    same = lambda i: (0, 0)
    block = lambda i: (i, 0)
    outs = (shaped(rows, own, dtype=BF16), shaped(rows, own), shaped(rank, own))
    return pl.pallas_call(
        finish,
        out_shape=outs,
        grid=(rows // step,),
        in_specs=[
            pl.BlockSpec(right.shape, lambda i: (0, 0, 0)),
            pl.BlockSpec(inverse.shape, same),
            pl.BlockSpec((step, 2 * rank), block),
            pl.BlockSpec((step, own), block),
        ],
        out_specs=(
            pl.BlockSpec((step, own), block),
            pl.BlockSpec((step, own), block),
            pl.BlockSpec((rank, own), same),
        ),
        scratch_shapes=[pltpu.VMEM((2 * rank, 2 * own), BF16)],
        cost_estimate=cost(6 * rows * rank * own, [right, left, merged] + list(outs)),
        compiler_params=pltpu.CompilerParams(vmem_limit_bytes=16 << 20),
    )(right, inverse, left, merged)


def direct(blocks, axes):
    return lax.all_to_all(blocks, axes, split_axis=0, concat_axis=0, tiled=True)


def shifted(value, across, shift):
    return lax.ppermute(value, "x", [(i, (i + shift) % across) for i in range(across)])


def after(value, earlier):
    return lax.optimization_barrier((value, earlier))[0]


def per_device(sizes, tokens_in, grad_out, error_old, q_prev):
    tokens, outgrad, memory = tokens_in[0], grad_out[0], error_old[0]
    count, rows = tokens.shape
    own, rank = q_prev.shape
    reps, across, deep = sizes["rep"], sizes["x"], sizes["z"]
    peers = reps * across
    width = rows * rank // (16 * peers)

    gathered = lax.all_gather(tokens, ("x", "z"), axis=0, tiled=True)
    q_t = q_prev.T
    cut = vmem_call(cut_columns, shaped(deep, across * 2, count, own, dtype=BF16), outgrad)
    q_t, memory = lax.optimization_barrier((q_t, memory, cut))[:2]
    cut = direct(cut, "z")
    q_pair = jnp.stack([q_t, lax.ppermute(q_t, "core", SWAP)])
    q_near = [q_pair] + [shifted(q_pair, across, s) for s in range(1, across)]
    left_own, memory_t = vmem_call(
        error_parts,
        (shaped(rank + count, rows), shaped(own, rows)),
        q_t,
        memory,
        tokens,
        flops=6 * rank * rows * own,
    )
    q_near = vmem_call(pack_factor, shaped(2 * across, 2 * rank, own, dtype=BF16), *q_near)
    projected = vmem_call(
        project,
        shaped(deep * 2, count // 2, own),
        q_near,
        cut,
        flops=4 * rank * own * deep * across * 2 * count,
    )
    left_own2 = lax.ppermute(after(left_own, projected), "core", SWAP)
    projected = direct(projected, ("z", "core"))
    left = vmem_call(
        token_left,
        shaped(peers, 8, width),
        projected,
        left_own,
        left_own2,
        flops=4 * rank * count * rows,
    )
    late_cut = after(cut, left)
    chip = shaped(deep, 2, count, own, dtype=BF16)
    columns = vmem_call(pick_columns, (chip,) * across, late_cut)
    columns = [columns[0]] + [shifted(columns[s], across, s) for s in range(1, across)]
    columns = vmem_call(
        turn_columns,
        shaped(2 * own, deep * across * count, dtype=BF16),
        *columns,
    )
    left = direct(left, PEERS)
    left = vmem_call(add_spread, shaped(deep, 8, width), after(left, columns))
    left = direct(left, "z")
    summed = vmem_call(add_spread, shaped(peers, 8, width), left)
    left = direct(summed, PEERS)
    gathered = after(gathered, left)
    grad_keep, grad_send = vmem_call(
        turned_grad,
        (shaped(own, rows), shaped(own, rows)),
        columns,
        memory_t,
        gathered,
        flops=4 * own * rows * deep * across * count,
    )
    grad_in = lax.ppermute(grad_send, "core", SWAP)

    left2 = lax.ppermute(left, "core", SWAP)

    left_wide, left_tall = vmem_call(
        left_forms, (shaped(2 * rank, rows, dtype=BF16), shaped(rows, 2 * rank, dtype=BF16)), left, left2
    )
    inverse = vmem_call(inverse_factor, shaped(rank, rank), left, left2, flops=12 * rank * rank * rows)
    merged_t, right = vmem_call(
        merge,
        (shaped(own, rows), shaped(reps, rank, own)),
        grad_keep,
        grad_in,
        left_wide,
        flops=6 * rank * own * rows,
    )
    right = direct(right, "rep")
    merged = vmem_call(turn, shaped(rows, own), merged_t)
    approx, new_error, q_new = finished(right, inverse, left_tall, merged)
    return approx, new_error[None], q_new.T


def solution(mesh):
    return build(mesh, (8, 4, 8, 2))


def build(mesh, shape):
    names = ("rep", "x", "z", "core")
    grid = Mesh(mesh.devices.reshape(shape), names)
    sizes = dict(zip(names, shape))
    shard = ("x", "z", "core")
    placed = (
        P("rep", shard, None),
        P("rep", shard, None),
        P("rep", None, shard),
        P(shard, None),
    )
    return jax.shard_map(
        lambda *args: per_device(sizes, *args),
        mesh=grid,
        in_specs=placed,
        out_specs=(P(None, shard), P("rep", None, shard), P(shard, None)),
        check_vma=False,
    )
```

```python
import jax
import jax.numpy as jnp
from jax import lax
from jax.experimental import pallas as pl
from jax.experimental.pallas import tpu as pltpu
from jax.sharding import Mesh, PartitionSpec as P

F32 = jnp.float32
BF16 = jnp.bfloat16
HIGHEST = lax.Precision.HIGHEST
PEERS = ("rep", "x")
SWAP = [(0, 1), (1, 0)]
LANES = 128


def split(value):
    high = value.astype(BF16)
    return high, (value - high.astype(F32)).astype(BF16)


def dot_nt(a, b, precision=None):
    return lax.dot_general(a, b, (((1,), (1,)), ((), ())), precision=precision, preferred_element_type=F32)


def dot_nn(a, b, precision=None):
    return lax.dot_general(a, b, (((1,), (0,)), ((), ())), precision=precision, preferred_element_type=F32)


def dot_tn(a, b, precision=None):
    return lax.dot_general(a, b, (((0,), (0,)), ((), ())), precision=precision, preferred_element_type=F32)


def shaped(*shape, dtype=F32):
    return jax.ShapeDtypeStruct(shape, dtype)


def size_of(value):
    count = value.dtype.itemsize
    for extent in value.shape:
        count *= extent
    return count


def cost(flops, values):
    return pl.CostEstimate(flops=flops, bytes_accessed=sum(size_of(v) for v in values), transcendentals=0)


def vmem_call(body, out_shape, *args, flops=0, scratch=(), extra=0):
    whole = pl.BlockSpec(memory_space=pltpu.VMEM)
    many = isinstance(out_shape, (tuple, list))
    values = list(args) + (list(out_shape) if many else [out_shape])
    room = sum(size_of(v) for v in values) + extra
    return pl.pallas_call(
        body,
        out_shape=out_shape,
        in_specs=[whole] * len(args),
        out_specs=tuple(whole for _ in out_shape) if many else whole,
        scratch_shapes=scratch,
        cost_estimate=cost(flops, values),
        compiler_params=pltpu.CompilerParams(vmem_limit_bytes=room + (6 << 20)),
    )(*args)


def steps_of(rows, step=512):
    step = min(rows, step)
    return [(start, step) for start in range(0, rows, step)]


def error_parts(q_ref, e_ref, tok_ref, left_ref, turned_ref):
    rank = q_ref.shape[0]
    q_high, q_low = split(q_ref[...])
    both = jnp.concatenate([q_high, q_low], axis=0)
    for start, step in steps_of(e_ref.shape[0]):
        cols = pl.ds(start, step)
        turned = e_ref[cols, :].T
        turned_ref[:, cols] = turned
        e_high, e_low = split(turned)
        wide = dot_nn(both, e_high)
        left_ref[:rank, cols] = wide[:rank] + (wide[rank:] + dot_nn(q_high, e_low))
        left_ref[rank:, cols] = tok_ref[:, cols].astype(F32)


def cut_columns(in_ref, out_ref):
    deep, across, _, own = out_ref.shape
    for z in range(deep):
        for i in range(across):
            x, core = divmod(i, 2)
            start = ((x * deep + z) * 2 + core) * own
            out_ref[z, i] = in_ref[:, start : start + own]


def pack_factor(*refs):
    *q_refs, out_ref = refs
    across, rank = len(q_refs), q_refs[0].shape[1]
    x, core = lax.axis_index("x"), lax.axis_index("core")
    for shift, q_ref in enumerate(q_refs):
        source = lax.rem(x + across - shift, across)
        for i in (0, 1):
            high, low = split(q_ref[i])
            place = 2 * source + (core if i == 0 else 1 - core)
            out_ref[place] = jnp.concatenate([high, low], axis=0)


def project(q_ref, cols_ref, out_ref):
    near, wide, own = q_ref.shape
    rank = wide // 2
    deep, _, count, _ = cols_ref.shape
    total = jnp.zeros((deep * count, wide), F32)
    for i in range(near):
        total += dot_nt(cols_ref[:, i].reshape(deep * count, own), q_ref[i])
    value = total + pltpu.roll(total, rank, 1)
    half = count // 2
    lane = lax.broadcasted_iota(jnp.int32, (half, 2 * rank), 1)
    for z in range(deep):
        top = value[z * count : z * count + half]
        low = value[z * count + half : (z + 1) * count]
        packed = jnp.where(lane < rank, top, low)
        out_ref[2 * z] = packed
        out_ref[2 * z + 1] = packed


def pick_columns(cols_ref, *out_refs):
    across = len(out_refs)
    x = lax.axis_index("x")
    for shift, out_ref in enumerate(out_refs):
        out_ref[...] = cols_ref[:, pl.ds(2 * lax.rem(x + shift, across), 2)]


def turn_columns(*refs):
    *in_refs, out_ref = refs
    deep, _, count, own = in_refs[0].shape
    across = len(in_refs)
    x, core = lax.axis_index("x"), lax.axis_index("core")
    for shift, in_ref in enumerate(in_refs):
        source = lax.rem(x + across - shift, across)
        cols = pl.ds(pl.multiple_of(source * (deep * count), deep * count), deep * count)
        for i in (0, 1):
            block = in_ref[:, core if i == 0 else 1 - core].reshape(deep * count, own)
            out_ref[i * own : (i + 1) * own, cols] = block.astype(F32).T.astype(BF16)


def token_left(y_ref, add_ref, add2_ref, out_ref):
    rank, rows = y_ref.shape[2] // 2, add_ref.shape[1]
    core = lax.axis_index("core")
    packed = [y_ref[i] for i in (0, 1)]
    for z in range(1, y_ref.shape[0] // 2):
        packed = [packed[i] + y_ref[2 * z + i] for i in (0, 1)]
    ordered = [jnp.where(core == i, packed[0], packed[1]) for i in (0, 1)]
    value = jnp.concatenate(
        [part for one in ordered for part in (one, pltpu.roll(one, rank, 1))], axis=0
    )
    high, low = split(value.T[:rank])
    both = jnp.concatenate([high, low], axis=0)
    bands = rank // 8
    blocks = out_ref.shape[0] // bands
    width = out_ref.shape[2]
    for c in range(blocks):
        cols = pl.ds(pl.multiple_of(core * (rows // 2) + c * width, LANES), width)
        pair = jnp.concatenate([add_ref[rank:, cols], add2_ref[rank:, cols]], axis=0).astype(BF16)
        wide = dot_nn(both, pair)
        total = (add_ref[:rank, cols] + add2_ref[:rank, cols]) + (wide[:rank] + wide[rank:])
        for b in range(bands):
            out_ref[b * blocks + c] = total[b * 8 : (b + 1) * 8]


def add_spread(in_ref, out_ref):
    total = jnp.sum(in_ref[...], axis=0)
    for i in range(out_ref.shape[0]):
        out_ref[i] = total


def unblock(left_ref, rank, c):
    bands = rank // 8
    blocks = left_ref.shape[0] // bands
    return jnp.concatenate([left_ref[b * blocks + c] for b in range(bands)], axis=0)


def left_forms(mine_ref, other_ref, wide_ref, tall_ref):
    rank = wide_ref.shape[0] // 2
    rows = wide_ref.shape[1]
    width = mine_ref.shape[2]
    core = lax.axis_index("core")
    for ref, place in ((mine_ref, core), (other_ref, 1 - core)):
        for c in range(rows // 2 // width):
            high, low = split(unblock(ref, rank, c))
            both = jnp.concatenate([high, low], axis=0)
            cols = pl.ds(pl.multiple_of(place * (rows // 2) + c * width, LANES), width)
            wide_ref[:, cols] = both
            tall_ref[cols, :] = both.astype(F32).T.astype(BF16)


def inverse_factor(mine_ref, other_ref, out_ref):
    rank = out_ref.shape[0]
    grams = []
    for ref in (mine_ref, other_ref):
        gram = jnp.zeros((rank, rank), F32)
        for c in range(ref.shape[0] // (rank // 8)):
            block = unblock(ref, rank, c)
            gram += dot_nt(block, block, HIGHEST)
        grams.append(gram)
    gram = grams[0] + grams[1]
    row_at = lax.broadcasted_iota(jnp.int32, (rank, rank), 0)
    col_at = lax.broadcasted_iota(jnp.int32, (rank, rank), 1)
    work = jnp.concatenate([gram, (row_at == col_at).astype(F32)], axis=1)
    tiles = [work[i * 8 : (i + 1) * 8] for i in range(rank // 8)]
    below = lax.broadcasted_iota(jnp.int32, (8, 1), 0)
    done = []
    for k in range(rank):
        at, sub = divmod(k, 8)
        row = tiles[at][sub : sub + 1, :]
        pivot = row[:, k : k + 1]
        scaled = row / pivot
        done.append(row * lax.rsqrt(pivot))
        for i in range(at, rank // 8):
            column = tiles[i][:, k : k + 1]
            if i == at:
                column = jnp.where(below > sub, column, 0.0)
            tiles[i] = tiles[i] - column * scaled
    out_ref[...] = jnp.concatenate(done, axis=0)[:, rank:]


def turned_grad(cols_ref, e_ref, tok_ref, keep_ref, send_ref):
    own = keep_ref.shape[0]
    for start, step in steps_of(tok_ref.shape[1]):
        cols = pl.ds(start, step)
        both = dot_nn(cols_ref[...], tok_ref[:, cols])
        send_ref[:, cols] = both[own:]
        keep_ref[:, cols] = both[:own] + e_ref[:, cols]


def merge(keep_ref, in_ref, left_ref, merged_ref, right_ref):
    rank = left_ref.shape[0] // 2
    own, rows = keep_ref.shape
    top = jnp.zeros((2 * rank, own), F32)
    low = jnp.zeros((rank, own), F32)
    for start, step in steps_of(rows):
        cols = pl.ds(start, step)
        merged = keep_ref[:, cols] + in_ref[:, cols]
        merged_ref[:, cols] = merged
        m_high, m_low = split(merged)
        top += dot_nt(left_ref[:, cols], m_high)
        low += dot_nt(left_ref[:rank, cols], m_low)
    right = top[:rank] + (top[rank:] + low)
    for g in range(right_ref.shape[0]):
        right_ref[g] = right


def turn(in_ref, out_ref):
    for start, step in steps_of(in_ref.shape[1]):
        out_ref[pl.ds(start, step), :] = in_ref[:, pl.ds(start, step)].T


def finish(right_ref, inverse_ref, left_ref, merged_ref, approx_ref, error_ref, q_ref, weights):
    rank, own = q_ref.shape
    reps = right_ref.shape[0]

    @pl.when(pl.program_id(0) == 0)
    def _():
        inverse = inverse_ref[...]
        right = jnp.sum(right_ref[...], axis=0)
        q_new = dot_nn(inverse, right, HIGHEST) / reps
        q_ref[...] = q_new
        high, low = split(dot_tn(inverse, q_new, HIGHEST))
        weights[:rank, :own] = high
        weights[rank:, :own] = high
        weights[:rank, own:] = low
        weights[rank:, own:] = jnp.zeros_like(low)

    wide = dot_nn(left_ref[...], weights[...])
    approx = wide[:, :own] + wide[:, own:]
    approx_ref[...] = approx.astype(BF16)
    error_ref[...] = merged_ref[...] - approx


def finished(right, inverse, left, merged):
    rows, own = merged.shape
    rank = inverse.shape[0]
    step = min(rows, 768)
    same = lambda i: (0, 0)
    block = lambda i: (i, 0)
    outs = (shaped(rows, own, dtype=BF16), shaped(rows, own), shaped(rank, own))
    return pl.pallas_call(
        finish,
        out_shape=outs,
        grid=(rows // step,),
        in_specs=[
            pl.BlockSpec(right.shape, lambda i: (0, 0, 0)),
            pl.BlockSpec(inverse.shape, same),
            pl.BlockSpec((step, 2 * rank), block),
            pl.BlockSpec((step, own), block),
        ],
        out_specs=(
            pl.BlockSpec((step, own), block),
            pl.BlockSpec((step, own), block),
            pl.BlockSpec((rank, own), same),
        ),
        scratch_shapes=[pltpu.VMEM((2 * rank, 2 * own), BF16)],
        cost_estimate=cost(6 * rows * rank * own, [right, left, merged] + list(outs)),
        compiler_params=pltpu.CompilerParams(vmem_limit_bytes=16 << 20),
    )(right, inverse, left, merged)


def direct(blocks, axes):
    return lax.all_to_all(blocks, axes, split_axis=0, concat_axis=0, tiled=True)


def shifted(value, across, shift):
    return lax.ppermute(value, "x", [(i, (i + shift) % across) for i in range(across)])


def after(value, earlier):
    return lax.optimization_barrier((value, earlier))[0]


def per_device(sizes, tokens_in, grad_out, error_old, q_prev):
    tokens, outgrad, memory = tokens_in[0], grad_out[0], error_old[0]
    count, rows = tokens.shape
    own, rank = q_prev.shape
    reps, across, deep = sizes["rep"], sizes["x"], sizes["z"]
    peers = reps * across
    width = rows * rank // (16 * peers)

    gathered = lax.all_gather(tokens, ("x", "z"), axis=0, tiled=True)
    q_t = q_prev.T
    cut = vmem_call(cut_columns, shaped(deep, across * 2, count, own, dtype=BF16), outgrad)
    q_t, memory = lax.optimization_barrier((q_t, memory, cut))[:2]
    cut = direct(cut, "z")
    q_pair = jnp.stack([q_t, lax.ppermute(q_t, "core", SWAP)])
    q_near = [q_pair] + [shifted(q_pair, across, s) for s in range(1, across)]
    left_own, memory_t = vmem_call(
        error_parts,
        (shaped(rank + count, rows), shaped(own, rows)),
        q_t,
        memory,
        tokens,
        flops=6 * rank * rows * own,
    )
    q_near = vmem_call(pack_factor, shaped(2 * across, 2 * rank, own, dtype=BF16), *q_near)
    projected = vmem_call(
        project,
        shaped(deep * 2, count // 2, own),
        q_near,
        cut,
        flops=4 * rank * own * deep * across * 2 * count,
    )
    left_own2 = lax.ppermute(after(left_own, projected), "core", SWAP)
    projected = direct(projected, ("z", "core"))
    left = vmem_call(
        token_left,
        shaped(peers, 8, width),
        projected,
        left_own,
        left_own2,
        flops=4 * rank * count * rows,
    )
    late_cut = after(cut, left)
    chip = shaped(deep, 2, count, own, dtype=BF16)
    columns = list(vmem_call(pick_columns, (chip,) * across, late_cut))
    far = across // 2
    near = [s for s in range(1, across) if s != far]
    for s in near:
        columns[s] = shifted(columns[s], across, s)
    left = direct(left, PEERS)
    left = after(left, [columns[s] for s in near])
    left = vmem_call(add_spread, shaped(deep, 8, width), left)
    columns[far] = shifted(after(columns[far], left), across, far)
    left = direct(left, "z")
    summed = vmem_call(add_spread, shaped(peers, 8, width), after(left, columns[far]))
    columns = vmem_call(
        turn_columns,
        shaped(2 * own, deep * across * count, dtype=BF16),
        *columns,
    )
    left = direct(summed, PEERS)
    gathered = after(gathered, left)
    grad_keep, grad_send = vmem_call(
        turned_grad,
        (shaped(own, rows), shaped(own, rows)),
        columns,
        memory_t,
        gathered,
        flops=4 * own * rows * deep * across * count,
    )
    grad_in = lax.ppermute(grad_send, "core", SWAP)

    left2 = lax.ppermute(left, "core", SWAP)

    left_wide, left_tall = vmem_call(
        left_forms, (shaped(2 * rank, rows, dtype=BF16), shaped(rows, 2 * rank, dtype=BF16)), left, left2
    )
    inverse = vmem_call(inverse_factor, shaped(rank, rank), left, left2, flops=12 * rank * rank * rows)
    merged_t, right = vmem_call(
        merge,
        (shaped(own, rows), shaped(reps, rank, own)),
        grad_keep,
        grad_in,
        left_wide,
        flops=6 * rank * own * rows,
    )
    right = direct(right, "rep")
    merged = vmem_call(turn, shaped(rows, own), merged_t)
    approx, new_error, q_new = finished(right, inverse, left_tall, merged)
    return approx, new_error[None], q_new.T


def solution(mesh):
    return build(mesh, (8, 4, 8, 2))


def build(mesh, shape):
    names = ("rep", "x", "z", "core")
    grid = Mesh(mesh.devices.reshape(shape), names)
    sizes = dict(zip(names, shape))
    shard = ("x", "z", "core")
    placed = (
        P("rep", shard, None),
        P("rep", shard, None),
        P("rep", None, shard),
        P(shard, None),
    )
    return jax.shard_map(
        lambda *args: per_device(sizes, *args),
        mesh=grid,
        in_specs=placed,
        out_specs=(P(None, shard), P("rep", None, shard), P(shard, None)),
        check_vma=False,
    )
```
